256 devices in a mesh: dp: 32 (over y, x, core), tensor: 8 (over z).
Axes of the slice: x: 4, y: 4, z: 8, core: 2. Of those that a mesh axis runs over, the one named last changes fastest.
Arguments:
- gate_pre: bfloat16 [4096, 14336], P('dp', 'tensor'), may hold values from -8 to 8
- up_pre: bfloat16 [4096, 14336], P('dp', 'tensor')
- w_down: float32 [14336, 8192], P('tensor', 'dp')
- out_grad: bfloat16 [4096, 8192], P('tensor', 'dp'), may hold values from -6 to 6
- outlier_ids: int32 [128], replicated, may hold values from 0 to 14335, as said below
Outputs:
- output: bfloat16 [4096, 8192], P('tensor', 'dp')
- weight_grad: float32 [14336, 8192], P('tensor', 'dp')
- gate_grad: bfloat16 [4096, 14336], P('dp', 'tensor')
- up_grad: bfloat16 [4096, 14336], P('dp', 'tensor')
The draws below stay inside these ranges and needn't reach their ends.
Inputs may be any that keep to these rules, and one draw needn't show every extreme that they name: `outlier_ids`: 128 distinct hidden channels; the first and the last channel are always among them.
All inputs are finite; a program needn't handle non-finite values.
Results may differ from the reference program's by a relative error of at most 0.035.
Values may be sent and summed in bfloat16 or wider, within the bound.
No kernel may reach another device: no remote copies, remote signals or barrier semaphores. Data moves between devices by JAX's collectives and lax.ppermute only.
A program may use at most 128 MiB of HBM per device.

```python
import math
import jax
import jax.numpy as jnp
from jax import lax

D = 8192
FF = 14336
OUTER_ORDER = 16
INNER_ORDER = 128
N_OUT = 128
TOKENS = 4096
N_DP = 32


special_gain = 8.0


extra_amplitude = 3.0


def special_channels(key):
    key = jax.random.fold_in(key, 37)
    middle = jax.random.permutation(key, FF - 2)[:N_OUT - 2].astype(jnp.int32) + 1
    ends = jnp.array([0, FF - 1], dtype=jnp.int32)
    return jnp.concatenate([ends, middle]).astype(jnp.int32)


def bit_parity(values, bit_count):
    parity = jnp.zeros(values.shape, jnp.int32)
    for section_bit in range(bit_count):
        parity = jnp.bitwise_xor(parity, jnp.bitwise_and(jnp.right_shift(values, section_bit), 1))
    return parity


def rotation_signs(chosen):
    inner = FF // (OUTER_ORDER * INNER_ORDER)
    columns = jnp.arange(FF, dtype=jnp.int32)
    outer_row = (chosen // (inner * INNER_ORDER))[:, None]
    outer_col = (columns // (inner * INNER_ORDER))[None, :]
    group_row = (chosen // INNER_ORDER % inner)[:, None]
    group_col = (columns // INNER_ORDER % inner)[None, :]
    inner_row = (chosen % INNER_ORDER)[:, None]
    inner_col = (columns % INNER_ORDER)[None, :]
    bit_count = max(OUTER_ORDER.bit_length(), INNER_ORDER.bit_length())
    parity = jnp.bitwise_xor(bit_parity(jnp.bitwise_and(outer_row, outer_col), bit_count), bit_parity(jnp.bitwise_and(inner_row, inner_col), bit_count))
    same_group = (group_row == group_col).astype(jnp.float32)
    return (1 - 2 * parity).astype(jnp.float32) * same_group


def draw_up_pre(key, part):
    chosen = special_channels(key)
    key = jax.random.fold_in(key, 11)
    base_key, row_key, col_key, coef_key = jax.random.split(key, 4)
    base_draw = jnp.clip(jax.random.normal(base_key, (TOKENS, FF), jnp.float32), -6.0, 6.0)
    row_scale = jnp.exp(jax.random.uniform(row_key, (TOKENS, 1), jnp.float32, -1.2, 1.2))
    col_scale = jnp.exp(jax.random.uniform(col_key, (1, FF), jnp.float32, -0.7, 0.7))
    picks = jax.random.randint(coef_key, (TOKENS, N_OUT), 0, 8)
    coefficients = jnp.where(picks < 4, picks - 4, picks - 3).astype(jnp.float32)
    signs = rotation_signs(chosen)
    extra = jnp.dot(coefficients, signs, precision=lax.Precision.HIGHEST)
    extra = extra * (extra_amplitude / math.sqrt(OUTER_ORDER * INNER_ORDER))
    return ((base_draw * col_scale + extra) * row_scale).astype(jnp.bfloat16)


def draw_w_down(key, part):
    chosen = special_channels(key)
    key = jax.random.fold_in(key, 23)
    base_key, rough_key = jax.random.split(key, 2)
    base_draw = jnp.clip(jax.random.normal(base_key, (FF, D), jnp.float32), -6.0, 6.0)
    rising = jnp.exp(jnp.linspace(-0.55, 0.55, FF, dtype=jnp.float32))[:, None]
    roughness = jnp.exp(jax.random.uniform(rough_key, (FF, 1), jnp.float32, -0.35, 0.35))
    channels = jnp.arange(FF, dtype=jnp.int32)
    marked = jnp.any(chosen[:, None] == channels[None, :], axis=0)
    row_gain = jnp.where(marked, special_gain, 1.0).astype(jnp.float32)[:, None]
    return base_draw * rising * roughness * row_gain * FF ** (-0.5)


def draw_outlier_ids(key, part):
    return special_channels(key)


def block_levels(stream_key, dims, cuts, smallest, largest):
    def one(axis_at, blocks):
        steps = jax.random.uniform(jax.random.fold_in(jax.random.fold_in(stream_key, 6), axis_at), (blocks,), jnp.float32, smallest / len(cuts), largest / len(cuts))
        return jnp.repeat(jnp.exp(steps), dims[axis_at] // blocks).reshape((-1,) + (1,) * (len(dims) - axis_at - 1))

    gain = one(*cuts[0])
    for cut in cuts[1:]:
        gain = gain * one(*cut)
    return gain


def noise(stream_key, extent, width, limit, pieces=(), kind=jnp.bfloat16):
    gain = block_levels(stream_key, extent, pieces, -0.22, 0.18) if pieces else 1.0
    values = jax.random.normal(stream_key, extent, jnp.float32) * width * gain
    return jnp.minimum(jnp.maximum(values, -limit), limit).astype(kind)


def setup_inputs(seed: int = 0) -> dict:
    arg_keys = jax.random.split(jax.random.key(seed), 6)
    gate_pre = noise(arg_keys[0], (TOKENS, FF), 1.5, 8.0, ((0, 32), (1, 8)))
    up_pre = draw_up_pre(jax.random.fold_in(arg_keys[5], 71), 0)
    w_down = draw_w_down(jax.random.fold_in(arg_keys[5], 71), 0)
    out_grad = noise(arg_keys[3], (TOKENS, D), 1.0, 6.0, ((0, 8), (1, 32)))
    outlier_ids = draw_outlier_ids(jax.random.fold_in(arg_keys[5], 71), 0)
    return dict(gate_pre=gate_pre, up_pre=up_pre, w_down=w_down, out_grad=out_grad, outlier_ids=outlier_ids)


softness = 0.5
levels = 7.0
epsilon = 1e-05
two_pi = 2.0 * math.pi

def sylvester(dimension):
    row_index = jnp.arange(dimension, dtype=jnp.int32)[:, None]
    col_index = jnp.arange(dimension, dtype=jnp.int32)[None, :]
    common = jnp.bitwise_and(row_index, col_index)
    parity = jnp.zeros((dimension, dimension), jnp.int32)
    for section_bit in range(max(dimension.bit_length() - 1, 0)):
        parity = jnp.bitwise_xor(parity, jnp.bitwise_and(jnp.right_shift(common, section_bit), 1))
    return (1 - 2 * parity).astype(jnp.float32)

def soften(values, scale):
    return values - softness * scale * jnp.sin(two_pi * values / scale) / two_pi

def soft_slope(values, scale):
    return 1.0 - softness * jnp.cos(two_pi * values / scale)

def rotate(values):
    token_count = values.shape[0]
    inner = FF // (OUTER_ORDER * INNER_ORDER)
    shaped = values.astype(jnp.float32).reshape(token_count, OUTER_ORDER, inner, INNER_ORDER)
    mixture = jnp.einsum('tsgc,dc->tsgd', shaped, sylvester(INNER_ORDER), precision=lax.Precision.HIGHEST)
    mixture = jnp.einsum('tsgd,rs->trgd', mixture, sylvester(OUTER_ORDER), precision=lax.Precision.HIGHEST)
    normalizer = 1.0 / math.sqrt(OUTER_ORDER * INNER_ORDER)
    return (mixture * normalizer).reshape(token_count, FF)

def reference(gate_pre, up_pre, w_down, out_grad, outlier_ids):
    gate_value = gate_pre.astype(jnp.float32)
    up_value = up_pre.astype(jnp.float32)
    sigmoid_gate = jax.nn.sigmoid(gate_value)
    silu_gate = gate_value * sigmoid_gate
    hidden = (silu_gate * up_value).astype(jnp.bfloat16)
    rotated = rotate(hidden)
    channels = jnp.arange(FF, dtype=jnp.int32)
    special = jnp.any(outlier_ids[:, None] == channels[None, :], axis=0)
    token_scale = (lax.optimization_barrier(jnp.max(jnp.where(special[None, :], 0.0, jnp.abs(rotated)), axis=1, keepdims=True)) + epsilon) / levels
    column_scale = (lax.optimization_barrier(jnp.max(jnp.where(special[:, None], 0.0, jnp.abs(w_down)), axis=0, keepdims=True)) + epsilon) / levels
    quant_act = jnp.where(special[None, :], rotated, soften(rotated, token_scale)).astype(jnp.bfloat16)
    quant_w = jnp.where(special[:, None], w_down, soften(w_down, column_scale)).astype(jnp.bfloat16)
    output = jnp.dot(quant_act, quant_w, preferred_element_type=jnp.float32).astype(jnp.bfloat16)
    raw_grad = jnp.dot(quant_act.T, out_grad, preferred_element_type=jnp.float32)
    weight_grad = raw_grad * jnp.where(special[:, None], 1.0, soft_slope(w_down, column_scale))
    block_width = D // N_DP

    def add_block(running, block_number):
        first_col = (block_number * block_width).astype(jnp.int32)
        grad_part = lax.dynamic_slice_in_dim(out_grad, first_col, block_width, 1)
        weight_part = lax.dynamic_slice_in_dim(quant_w, first_col, block_width, 1)
        term = lax.dot_general(grad_part, weight_part, (((1,), (1,)), ((), ())), preferred_element_type=jnp.float32)
        rounded = lax.optimization_barrier(term.astype(jnp.bfloat16))
        return (running + rounded.astype(jnp.float32), None)
    act_grad, unused = lax.scan(add_block, jnp.zeros((TOKENS, FF), jnp.float32), jnp.arange(N_DP, dtype=jnp.int32))
    rot_grad = (act_grad * jnp.where(special[None, :], 1.0, soft_slope(rotated, token_scale))).astype(jnp.bfloat16)
    hidden_grad = rotate(rot_grad)
    silu_slope = sigmoid_gate * (1.0 + gate_value * (1.0 - sigmoid_gate))
    gate_grad = (hidden_grad * up_value * silu_slope).astype(jnp.bfloat16)
    up_grad = (hidden_grad * silu_gate).astype(jnp.bfloat16)
    return (output, weight_grad, gate_grad, up_grad)
```

```python
import math

import jax
import jax.numpy as jnp
import numpy as np
from jax import lax
from jax.sharding import Mesh
from jax.sharding import PartitionSpec as P

OUTER_ORDER = 16
INNER_ORDER = 128
NY, NX, NC, NZ = 4, 4, 2, 8

softness = 0.5
levels = 7.0
epsilon = 1e-05
two_pi = 2.0 * math.pi
norm = 1.0 / math.sqrt(OUTER_ORDER * INNER_ORDER)
bf16, f32 = jnp.bfloat16, jnp.float32


def sylvester(n):
    i = np.arange(n)
    common = i[:, None] & i[None, :]
    parity = np.zeros((n, n), np.int64)
    while common.any():
        parity ^= common & 1
        common >>= 1
    return (1 - 2 * parity).astype(np.float32)


def fitted(function, terms):
    t = 0.125 * (1.0 - np.cos(np.pi * (np.arange(400) + 0.5) / 400.0))
    values = function(np.sqrt(t))
    basis = np.polynomial.chebyshev.Chebyshev.fit(t, values, terms - 1, domain=[0.0, 0.25])
    return [float(c) for c in basis.convert(kind=np.polynomial.Polynomial).coef]


SIN = fitted(lambda f: np.sin(two_pi * f) / f, 7)
COS = fitted(lambda f: np.cos(two_pi * f), 8)


def horner(coefficients, t):
    total = jnp.full_like(t, coefficients[-1])
    for c in coefficients[-2::-1]:
        total = total * t + c
    return total


def soft_pair(values, scale, inverse):
    turns = values * inverse
    turns = turns - jnp.floor(turns + 0.5)
    t = turns * turns
    softened = values - (softness / two_pi) * scale * (turns * horner(SIN, t))
    return softened, 1.0 - softness * horner(COS, t)


def shift(value, axis, size, step):
    return lax.ppermute(value, axis, [((i + step) % size, i) for i in range(size)])


def rolled(value, places):
    size = value.shape[0]
    twice = jnp.concatenate([value, value], axis=0)
    return lax.dynamic_slice_in_dim(twice, lax.rem(places, size), size, 0)


def mixed(value, table):
    inner = value.shape[1] // (2 * INNER_ORDER)
    value = value.reshape(NZ, 16, 2, inner, INNER_ORDER).transpose(1, 3, 0, 2, 4)
    value = value.reshape(16 * inner, OUTER_ORDER * INNER_ORDER)
    value = jnp.dot(value, table, preferred_element_type=f32) * norm
    return value.reshape(16, inner, OUTER_ORDER * INNER_ORDER)


def to_shards(value):
    inner = value.shape[1]
    value = value.reshape(16, inner, NZ, 2, INNER_ORDER).transpose(2, 0, 3, 1, 4)
    return value.reshape(NZ * 16, 2 * inner * INNER_ORDER)


def to_tokens(gate_pre, up_pre, column_local):
    gate_value = gate_pre.astype(f32)
    hidden = (gate_value * jax.nn.sigmoid(gate_value) * up_pre.astype(f32)).astype(bf16)
    count = column_local.shape[0] // INNER_ORDER
    digits = []
    rest = column_local
    for _ in range(3):
        digit = lax.reduce_precision(rest, 8, 7)
        digits.append(digit.reshape(count, INNER_ORDER))
        rest = rest - digit
    digits = jnp.concatenate(digits, axis=0).astype(bf16)
    digits = jnp.pad(digits, ((0, 16 - 3 * count), (0, 0)))
    digits = jnp.broadcast_to(digits[None], (NZ, 16, INNER_ORDER)).reshape(-1, INNER_ORDER)
    sent = jnp.concatenate([hidden, digits], axis=1)
    sent = lax.all_to_all(sent, "z", 0, 0, tiled=True)
    got = sent.reshape(NZ, 16, -1)[:, : 3 * count, hidden.shape[1] :].astype(f32)
    got = got.reshape(NZ, 3, count * INNER_ORDER)
    return got[:, 0] + got[:, 1] + got[:, 2], sent


def local(gate_pre, up_pre, w_down, out_grad, outlier_ids):
    tok_rows, width = gate_pre.shape
    columns = w_down.shape[1]
    inner = width // (2 * INNER_ORDER)
    y, x, c, z = (lax.axis_index(a) for a in ("y", "x", "c", "z"))
    first = lax.shift_right_logical(x, 1) == 0
    even = c == 0
    table = jnp.asarray(np.kron(sylvester(OUTER_ORDER), sylvester(INNER_ORDER)), bf16)

    lanes = jnp.arange(INNER_ORDER, dtype=jnp.int32)
    groups = jnp.arange(NZ * width // INNER_ORDER, dtype=jnp.int32)
    high = (groups[:, None] == (outlier_ids // INNER_ORDER)[None, :]).astype(bf16)
    low = ((outlier_ids % INNER_ORDER)[:, None] == lanes[None, :]).astype(bf16)
    special = jnp.dot(high, low, preferred_element_type=f32)
    special_rows = lax.dynamic_index_in_dim(special.reshape(NZ, width), z, 0, keepdims=False)
    special_rows = special_rows.reshape(width, 1)
    special_mixed = special.reshape(NZ, 2, inner, INNER_ORDER).transpose(2, 0, 1, 3)
    special_mixed = special_mixed.reshape(1, inner, OUTER_ORDER * INNER_ORDER) != 0.0

    column_local = jnp.max(jnp.where(special_rows == 0.0, jnp.abs(w_down), 0.0), axis=0)
    peaks, sent = to_tokens(gate_pre, up_pre, column_local)

    own_grad = out_grad.reshape(2, 2, 2, 64, columns).transpose(2, 0, 1, 3, 4)
    own_grad = own_grad.reshape(8, 64, columns)
    own_grad, sent = lax.optimization_barrier((own_grad, sent))
    own_grad = lax.all_to_all(own_grad, ("x", "c"), split_axis=0, concat_axis=0, tiled=True)
    own_grad = rolled(own_grad.reshape(NX, NC, 64, columns), x)
    near_grad = jnp.where(even, own_grad[:, 0], own_grad[:, 1])
    far_grad = jnp.where(even, own_grad[:, 1], own_grad[:, 0])
    own_grad = jnp.concatenate([near_grad, far_grad], axis=0)
    own_grad = own_grad.transpose(1, 0, 2).reshape(64, 8 * columns)

    column_scale = ((jnp.max(peaks, axis=0) + epsilon) / levels)[None, :]
    softened, slope_w = soft_pair(w_down, column_scale, 1.0 / column_scale)
    quant_w = jnp.where(special_rows == 0.0, softened, w_down).astype(bf16)
    slope_w = jnp.where(special_rows == 0.0, slope_w, 1.0)
    sent, quant_w, own_grad = lax.optimization_barrier((sent, quant_w, own_grad))
    near = [quant_w] + [shift(quant_w, "x", NX, d) for d in (1, 2, 3)]
    near_w = jnp.concatenate(near, axis=1)
    far_w = shift(near_w, "c", NC, 1)

    half = 4 * columns
    ups, downs = [own_grad], [own_grad]
    for _ in range(3):
        ups.append(shift(ups[-1], "z", NZ, 1))
        downs.append(shift(downs[-1], "z", NZ, -1))
    middle = jnp.concatenate(
        [shift(ups[3][:, :half], "z", NZ, 1), shift(downs[3][:, half:], "z", NZ, -1)], axis=1
    )
    held_grad = jnp.concatenate([*ups, middle, downs[3], downs[2], downs[1]], axis=0)

    rotated = mixed(sent[:, :width], table)
    token_peak = jnp.max(
        jnp.where(special_mixed, 0.0, jnp.abs(rotated)), axis=(1, 2), keepdims=True
    )
    token_scale = (token_peak + epsilon) / levels
    softened, slope_act = soft_pair(rotated, token_scale, 1.0 / token_scale)
    quant_act = jnp.where(special_mixed, rotated, softened).astype(bf16)
    slope_act = jnp.where(special_mixed, 1.0, slope_act)
    quant_act = lax.all_to_all(to_shards(quant_act), "z", 0, 0, tiled=True)
    quant_act = quant_act.reshape(2, 64, width)
    quant_act, _, _ = lax.optimization_barrier((quant_act, near, (ups, downs)))

    pairs = [(i, i ^ 2) for i in range(NX)]
    mine = jnp.where(first, quant_act[0], quant_act[1])
    other = lax.ppermute(jnp.where(first, quant_act[1], quant_act[0]), "x", pairs)
    mine, other = jnp.where(first, mine, other), jnp.where(first, other, mine)
    joined = jnp.concatenate([mine, other], axis=0)
    acts = [joined] + [shift(joined, "y", NY, d) for d in (1, 2, 3)]
    acts = jnp.concatenate(acts, axis=0).reshape(NZ, 64, width)
    acts = rolled(acts, z + NZ - 2 * y).reshape(512, width)

    rows_by_rows = (((1,), (1,)), ((), ()))
    share = lax.dot_general(
        held_grad[:, :half], near_w, rows_by_rows, preferred_element_type=f32
    ) + lax.dot_general(
        held_grad[:, half:], far_w, rows_by_rows, preferred_element_type=f32
    )
    share = share.astype(bf16)
    acts, share = lax.optimization_barrier((acts, share))
    share = rolled(share.reshape(NZ, 64, width), NZ - z).reshape(NY, 128, width)
    parts = []
    for cut in (slice(half, None), slice(0, half)):
        part = lax.dot_general(
            acts, held_grad[:, cut], (((0,), (0,)), ((), ())), preferred_element_type=f32
        )
        parts.append(part.astype(bf16))
    far_part, near_part = shift(parts[0], "c", NC, 1), parts[1]
    acts, near_part = lax.optimization_barrier((acts, near_part))

    partial = jnp.concatenate(
        [jnp.dot(acts, w, preferred_element_type=f32).astype(bf16) for w in (near_w, far_w)],
        axis=1,
    )
    partial = partial.reshape(NZ, 64, 8 * columns)
    cuts = [slice(d * columns, (d + 1) * columns) for d in range(4)]
    terms = [
        (near_part[:, cut].astype(f32) + far_part[:, cut].astype(f32)).astype(bf16)
        for cut in cuts[1:]
    ]
    partial, terms = lax.optimization_barrier((partial, terms))
    terms = [shift(term, "x", NX, -d) for d, term in zip((1, 2, 3), terms)]

    share = lax.all_to_all(share, "y", 0, 0, tiled=True).astype(f32)
    total = (share[0] + share[1] + share[2] + share[3]).astype(bf16).reshape(2, 64, width)
    mine = jnp.where(first, total[0], total[1])
    other = lax.ppermute(jnp.where(first, total[1], total[0]), "x", pairs)
    mine, other = jnp.where(first, mine, other), jnp.where(first, other, mine)
    act_grad = jnp.concatenate([mine, other], axis=0)
    act_grad = lax.all_to_all(act_grad, "z", 0, 0, tiled=True)
    act_grad, terms[0] = lax.optimization_barrier((act_grad, terms[0]))
    act_grad = act_grad.reshape(NZ, 16, 2, inner, INNER_ORDER).transpose(1, 3, 0, 2, 4)
    act_grad = act_grad.reshape(16, inner, OUTER_ORDER * INNER_ORDER).astype(f32)
    rot_grad = (act_grad * slope_act).astype(bf16)
    rot_grad = rot_grad.reshape(16 * inner, OUTER_ORDER * INNER_ORDER)
    hidden_grad = jnp.dot(rot_grad, table, preferred_element_type=f32) * norm
    hidden_grad = to_shards(hidden_grad.astype(bf16).reshape(16, inner, -1))

    low_part = shift(partial[4][:, :half], "z", NZ, -1).astype(f32)
    high_part = shift(partial[4][:, half:], "z", NZ, 1).astype(f32)
    zero = jnp.zeros_like(low_part)
    below = jnp.concatenate([low_part, zero], axis=1)
    above = jnp.concatenate([zero, high_part], axis=1)
    for d in (3, 2, 1):
        below = shift((partial[d].astype(f32) + below).astype(bf16), "z", NZ, -1).astype(f32)
        above = shift((partial[8 - d].astype(f32) + above).astype(bf16), "z", NZ, 1).astype(f32)
    output = (partial[0].astype(f32) + below + above).astype(bf16)
    output = output.reshape(64, 8, columns).transpose(1, 0, 2)
    near_out, far_out = output[:4], output[4:]
    output = jnp.stack(
        [jnp.where(even, near_out, far_out), jnp.where(even, far_out, near_out)], axis=1
    )
    output = rolled(output, NX - x).reshape(8, 64, columns)
    output = lax.all_to_all(output, ("x", "c"), split_axis=0, concat_axis=0, tiled=True)
    output = output.reshape(2, 2, 2, 64, columns).transpose(1, 2, 0, 3, 4).reshape(512, columns)

    hidden_grad, terms = lax.optimization_barrier((hidden_grad, terms))
    hidden_grad = lax.all_to_all(hidden_grad, "z", 0, 0, tiled=True).astype(f32)
    gate_value = gate_pre.astype(f32)
    sigmoid_gate = jax.nn.sigmoid(gate_value)
    silu_slope = sigmoid_gate * (1.0 + gate_value * (1.0 - sigmoid_gate))
    gate_grad = (hidden_grad * up_pre.astype(f32) * silu_slope).astype(bf16)
    up_grad = (hidden_grad * (gate_value * sigmoid_gate)).astype(bf16)
    raw = near_part[:, cuts[0]].astype(f32) + far_part[:, cuts[0]].astype(f32)
    for term in terms:
        raw = raw + term.astype(f32)
    weight_grad = raw * slope_w
    return (output, weight_grad, gate_grad, up_grad)


def solution(mesh):
    grid = Mesh(mesh.devices.reshape(NY, NX, NC, NZ), ("y", "x", "c", "z"))
    rows, cols = P(("y", "x", "c"), "z"), P("z", ("y", "x", "c"))
    return jax.shard_map(
        local,
        mesh=grid,
        in_specs=(rows, rows, cols, cols, P()),
        out_specs=(cols, cols, rows, rows),
        check_vma=False,
    )
```

```python
import math

import jax
import jax.numpy as jnp
import numpy as np
from jax import lax
from jax.sharding import Mesh
from jax.sharding import PartitionSpec as P

OUTER_ORDER = 16
INNER_ORDER = 128
NY, NX, NC, NZ = 4, 4, 2, 8

softness = 0.5
levels = 7.0
epsilon = 1e-05
two_pi = 2.0 * math.pi
norm = 1.0 / math.sqrt(OUTER_ORDER * INNER_ORDER)
bf16, f32 = jnp.bfloat16, jnp.float32


def sylvester(n):
    i = np.arange(n)
    common = i[:, None] & i[None, :]
    parity = np.zeros((n, n), np.int64)
    while common.any():
        parity ^= common & 1
        common >>= 1
    return (1 - 2 * parity).astype(np.float32)


def fitted(function, terms):
    t = 0.125 * (1.0 - np.cos(np.pi * (np.arange(400) + 0.5) / 400.0))
    values = function(np.sqrt(t))
    basis = np.polynomial.chebyshev.Chebyshev.fit(t, values, terms - 1, domain=[0.0, 0.25])
    return [float(c) for c in basis.convert(kind=np.polynomial.Polynomial).coef]


SIN = fitted(lambda f: np.sin(two_pi * f) / f, 7)
COS = fitted(lambda f: np.cos(two_pi * f), 8)


def horner(coefficients, t):
    total = jnp.full_like(t, coefficients[-1])
    for c in coefficients[-2::-1]:
        total = total * t + c
    return total


def soft_pair(values, scale, inverse):
    turns = values * inverse
    turns = turns - jnp.floor(turns + 0.5)
    t = turns * turns
    softened = values - (softness / two_pi) * scale * (turns * horner(SIN, t))
    return softened, 1.0 - softness * horner(COS, t)


def shift(value, axis, size, step):
    return lax.ppermute(value, axis, [((i + step) % size, i) for i in range(size)])


def rolled(value, places):
    size = value.shape[0]
    twice = jnp.concatenate([value, value], axis=0)
    return lax.dynamic_slice_in_dim(twice, lax.rem(places, size), size, 0)


def mixed(value, table):
    inner = value.shape[1] // (2 * INNER_ORDER)
    value = value.reshape(NZ, 16, 2, inner, INNER_ORDER).transpose(1, 3, 0, 2, 4)
    value = value.reshape(16 * inner, OUTER_ORDER * INNER_ORDER)
    value = jnp.dot(value, table, preferred_element_type=f32) * norm
    return value.reshape(16, inner, OUTER_ORDER * INNER_ORDER)


def to_shards(value):
    inner = value.shape[1]
    value = value.reshape(16, inner, NZ, 2, INNER_ORDER).transpose(2, 0, 3, 1, 4)
    return value.reshape(NZ * 16, 2 * inner * INNER_ORDER)


def to_tokens(gate_pre, up_pre, column_local):
    gate_value = gate_pre.astype(f32)
    hidden = (gate_value * jax.nn.sigmoid(gate_value) * up_pre.astype(f32)).astype(bf16)
    count = column_local.shape[0] // INNER_ORDER
    digits = []
    rest = column_local
    for _ in range(3):
        digit = lax.reduce_precision(rest, 8, 7)
        digits.append(digit.reshape(count, INNER_ORDER))
        rest = rest - digit
    digits = jnp.concatenate(digits, axis=0).astype(bf16)
    digits = jnp.pad(digits, ((0, 16 - 3 * count), (0, 0)))
    digits = jnp.broadcast_to(digits[None], (NZ, 16, INNER_ORDER)).reshape(-1, INNER_ORDER)
    sent = jnp.concatenate([hidden, digits], axis=1)
    sent = lax.all_to_all(sent, "z", 0, 0, tiled=True)
    got = sent.reshape(NZ, 16, -1)[:, : 3 * count, hidden.shape[1] :].astype(f32)
    got = got.reshape(NZ, 3, count * INNER_ORDER)
    return got[:, 0] + got[:, 1] + got[:, 2], sent


def local(gate_pre, up_pre, w_down, out_grad, outlier_ids):
    tok_rows, width = gate_pre.shape
    columns = w_down.shape[1]
    inner = width // (2 * INNER_ORDER)
    y, x, c, z = (lax.axis_index(a) for a in ("y", "x", "c", "z"))
    first = lax.shift_right_logical(x, 1) == 0
    even = c == 0
    table = jnp.asarray(np.kron(sylvester(OUTER_ORDER), sylvester(INNER_ORDER)), bf16)

    lanes = jnp.arange(INNER_ORDER, dtype=jnp.int32)
    groups = jnp.arange(NZ * width // INNER_ORDER, dtype=jnp.int32)
    high = (groups[:, None] == (outlier_ids // INNER_ORDER)[None, :]).astype(bf16)
    low = ((outlier_ids % INNER_ORDER)[:, None] == lanes[None, :]).astype(bf16)
    special = jnp.dot(high, low, preferred_element_type=f32)
    special_rows = lax.dynamic_index_in_dim(special.reshape(NZ, width), z, 0, keepdims=False)
    special_rows = special_rows.reshape(width, 1)
    special_mixed = special.reshape(NZ, 2, inner, INNER_ORDER).transpose(2, 0, 1, 3)
    special_mixed = special_mixed.reshape(1, inner, OUTER_ORDER * INNER_ORDER) != 0.0

    column_local = jnp.max(jnp.where(special_rows == 0.0, jnp.abs(w_down), 0.0), axis=0)
    peaks, sent = to_tokens(gate_pre, up_pre, column_local)

    own_grad = out_grad.reshape(2, 2, 2, 64, columns).transpose(2, 0, 1, 3, 4)
    own_grad = own_grad.reshape(8, 64, columns)
    own_grad, sent = lax.optimization_barrier((own_grad, sent))
    own_grad = lax.all_to_all(own_grad, ("x", "c"), split_axis=0, concat_axis=0, tiled=True)
    own_grad = rolled(own_grad.reshape(NX, NC, 64, columns), x)
    near_grad = jnp.where(even, own_grad[:, 0], own_grad[:, 1])
    far_grad = jnp.where(even, own_grad[:, 1], own_grad[:, 0])
    own_grad = jnp.concatenate([near_grad, far_grad], axis=0)
    own_grad = own_grad.transpose(1, 0, 2).reshape(64, 8 * columns)

    column_scale = ((jnp.max(peaks, axis=0) + epsilon) / levels)[None, :]
    softened, slope_w = soft_pair(w_down, column_scale, 1.0 / column_scale)
    quant_w = jnp.where(special_rows == 0.0, softened, w_down).astype(bf16)
    slope_w = jnp.where(special_rows == 0.0, slope_w, 1.0)
    sent, quant_w, own_grad = lax.optimization_barrier((sent, quant_w, own_grad))
    near = [quant_w] + [shift(quant_w, "x", NX, d) for d in (1, 2, 3)]
    near_w = jnp.concatenate(near, axis=1)
    far_w = shift(near_w, "c", NC, 1)

    half = 4 * columns
    ups, downs = [own_grad], [own_grad]
    for _ in range(3):
        ups.append(shift(ups[-1], "z", NZ, 1))
        downs.append(shift(downs[-1], "z", NZ, -1))
    middle = jnp.concatenate(
        [shift(ups[3][:, :half], "z", NZ, 1), shift(downs[3][:, half:], "z", NZ, -1)], axis=1
    )
    held_grad = jnp.concatenate([*ups, middle, downs[3], downs[2], downs[1]], axis=0)

    rotated = mixed(sent[:, :width], table)
    token_peak = jnp.max(
        jnp.where(special_mixed, 0.0, jnp.abs(rotated)), axis=(1, 2), keepdims=True
    )
    token_scale = (token_peak + epsilon) / levels
    softened, slope_act = soft_pair(rotated, token_scale, 1.0 / token_scale)
    quant_act = jnp.where(special_mixed, rotated, softened).astype(bf16)
    slope_act = jnp.where(special_mixed, 1.0, slope_act)
    quant_act = lax.all_to_all(to_shards(quant_act), "z", 0, 0, tiled=True)
    quant_act = quant_act.reshape(2, 64, width)
    quant_act, _, _ = lax.optimization_barrier((quant_act, near, (ups, downs)))

    pairs = [(i, i ^ 2) for i in range(NX)]
    mine = jnp.where(first, quant_act[0], quant_act[1])
    other = lax.ppermute(jnp.where(first, quant_act[1], quant_act[0]), "x", pairs)
    mine, other = jnp.where(first, mine, other), jnp.where(first, other, mine)
    joined = jnp.concatenate([mine, other], axis=0)
    rows_by_rows = (((1,), (1,)), ((), ()))
    share = lax.dot_general(
        held_grad[:, :half], near_w, rows_by_rows, preferred_element_type=f32
    ) + lax.dot_general(
        held_grad[:, half:], far_w, rows_by_rows, preferred_element_type=f32
    )
    share = share.astype(bf16)
    share = rolled(share.reshape(NZ, 64, width), NZ - z).reshape(NY, 128, width)
    share = lax.all_to_all(share, "y", 0, 0, tiled=True)
    late, share = lax.optimization_barrier((joined, share))
    acts = [joined, shift(joined, "y", NY, 1), shift(late, "y", NY, 2), shift(joined, "y", NY, 3)]
    acts = jnp.concatenate(acts, axis=0).reshape(NZ, 64, width)
    acts = rolled(acts, z + NZ - 2 * y).reshape(512, width)

    share = share.astype(f32)
    total = (share[0] + share[1] + share[2] + share[3]).astype(bf16).reshape(2, 64, width)
    mine = jnp.where(first, total[0], total[1])
    other = lax.ppermute(jnp.where(first, total[1], total[0]), "x", pairs)
    mine, other = jnp.where(first, mine, other), jnp.where(first, other, mine)
    act_grad = jnp.concatenate([mine, other], axis=0)
    acts, act_grad = lax.optimization_barrier((acts, act_grad))
    act_grad = lax.all_to_all(act_grad, "z", 0, 0, tiled=True)

    parts = []
    for cut in (slice(half, None), slice(0, half)):
        part = lax.dot_general(
            acts, held_grad[:, cut], (((0,), (0,)), ((), ())), preferred_element_type=f32
        )
        parts.append(part.astype(bf16))
    far_part, near_part = shift(parts[0], "c", NC, 1), parts[1]
    acts, near_part = lax.optimization_barrier((acts, near_part))

    partial = jnp.concatenate(
        [jnp.dot(acts, w, preferred_element_type=f32).astype(bf16) for w in (near_w, far_w)],
        axis=1,
    )
    partial = partial.reshape(NZ, 64, 8 * columns)
    cuts = [slice(d * columns, (d + 1) * columns) for d in range(4)]
    terms = [
        (near_part[:, cut].astype(f32) + far_part[:, cut].astype(f32)).astype(bf16)
        for cut in cuts[1:]
    ]
    partial, terms, act_grad = lax.optimization_barrier((partial, terms, act_grad))
    terms = [shift(term, "x", NX, -d) for d, term in zip((1, 2, 3), terms)]

    act_grad = act_grad.reshape(NZ, 16, 2, inner, INNER_ORDER).transpose(1, 3, 0, 2, 4)
    act_grad = act_grad.reshape(16, inner, OUTER_ORDER * INNER_ORDER).astype(f32)
    rot_grad = (act_grad * slope_act).astype(bf16)
    rot_grad = rot_grad.reshape(16 * inner, OUTER_ORDER * INNER_ORDER)
    hidden_grad = jnp.dot(rot_grad, table, preferred_element_type=f32) * norm
    hidden_grad = to_shards(hidden_grad.astype(bf16).reshape(16, inner, -1))

    low_part = shift(partial[4][:, :half], "z", NZ, -1).astype(f32)
    high_part = shift(partial[4][:, half:], "z", NZ, 1).astype(f32)
    zero = jnp.zeros_like(low_part)
    below = jnp.concatenate([low_part, zero], axis=1)
    above = jnp.concatenate([zero, high_part], axis=1)
    for d in (3, 2, 1):
        below = (partial[d].astype(f32) + below).astype(bf16)
        if d == 2:
            below, hidden_grad = lax.optimization_barrier((below, hidden_grad))
            hidden_grad = lax.all_to_all(hidden_grad, "z", 0, 0, tiled=True)
        if d < 3:
            below, terms[2 - 2 * (d - 1)] = lax.optimization_barrier(
                (below, terms[2 - 2 * (d - 1)])
            )
        below = shift(below, "z", NZ, -1).astype(f32)
        above = shift((partial[8 - d].astype(f32) + above).astype(bf16), "z", NZ, 1).astype(f32)
    output = (partial[0].astype(f32) + below + above).astype(bf16)
    output = output.reshape(64, 8, columns).transpose(1, 0, 2)
    near_out, far_out = output[:4], output[4:]
    output = jnp.stack(
        [jnp.where(even, near_out, far_out), jnp.where(even, far_out, near_out)], axis=1
    )
    output = rolled(output, NX - x).reshape(8, 64, columns)
    output, hidden_grad, terms[1] = lax.optimization_barrier((output, hidden_grad, terms[1]))
    hidden_grad = hidden_grad.astype(f32)
    output = lax.all_to_all(output, ("x", "c"), split_axis=0, concat_axis=0, tiled=True)
    output = output.reshape(2, 2, 2, 64, columns).transpose(1, 2, 0, 3, 4).reshape(512, columns)

    gate_value = gate_pre.astype(f32)
    sigmoid_gate = jax.nn.sigmoid(gate_value)
    silu_slope = sigmoid_gate * (1.0 + gate_value * (1.0 - sigmoid_gate))
    gate_grad = (hidden_grad * up_pre.astype(f32) * silu_slope).astype(bf16)
    up_grad = (hidden_grad * (gate_value * sigmoid_gate)).astype(bf16)
    raw = near_part[:, cuts[0]].astype(f32) + far_part[:, cuts[0]].astype(f32)
    for term in terms:
        raw = raw + term.astype(f32)
    weight_grad = raw * slope_w
    return (output, weight_grad, gate_grad, up_grad)


def solution(mesh):
    grid = Mesh(mesh.devices.reshape(NY, NX, NC, NZ), ("y", "x", "c", "z"))
    rows, cols = P(("y", "x", "c"), "z"), P("z", ("y", "x", "c"))
    return jax.shard_map(
        local,
        mesh=grid,
        in_specs=(rows, rows, cols, cols, P()),
        out_specs=(cols, cols, rows, rows),
        check_vma=False,
    )
```

```python
import math

import jax
import jax.numpy as jnp
import numpy as np
from jax import lax
from jax.sharding import Mesh
from jax.sharding import PartitionSpec as P

OUTER_ORDER = 16
INNER_ORDER = 128
NY, NX, NC, NZ = 4, 4, 2, 8

softness = 0.5
levels = 7.0
epsilon = 1e-05
two_pi = 2.0 * math.pi
norm = 1.0 / math.sqrt(OUTER_ORDER * INNER_ORDER)
bf16, f32 = jnp.bfloat16, jnp.float32


def sylvester(n):
    i = np.arange(n)
    common = i[:, None] & i[None, :]
    parity = np.zeros((n, n), np.int64)
    while common.any():
        parity ^= common & 1
        common >>= 1
    return (1 - 2 * parity).astype(np.float32)


def fitted(function, terms):
    t = 0.125 * (1.0 - np.cos(np.pi * (np.arange(400) + 0.5) / 400.0))
    values = function(np.sqrt(t))
    basis = np.polynomial.chebyshev.Chebyshev.fit(t, values, terms - 1, domain=[0.0, 0.25])
    return [float(c) for c in basis.convert(kind=np.polynomial.Polynomial).coef]


SIN = fitted(lambda f: np.sin(two_pi * f) / f, 7)
COS = fitted(lambda f: np.cos(two_pi * f), 8)


def horner(coefficients, t):
    total = jnp.full_like(t, coefficients[-1])
    for c in coefficients[-2::-1]:
        total = total * t + c
    return total


def soft_pair(values, scale, inverse):
    turns = values * inverse
    turns = turns - jnp.floor(turns + 0.5)
    t = turns * turns
    softened = values - (softness / two_pi) * scale * (turns * horner(SIN, t))
    return softened, 1.0 - softness * horner(COS, t)


def shift(value, axis, size, step):
    return lax.ppermute(value, axis, [((i + step) % size, i) for i in range(size)])


def rolled(value, places):
    size = value.shape[0]
    twice = jnp.concatenate([value, value], axis=0)
    return lax.dynamic_slice_in_dim(twice, lax.rem(places, size), size, 0)


def mixed(value, table):
    inner = value.shape[1] // (2 * INNER_ORDER)
    value = value.reshape(NZ, 16, 2, inner, INNER_ORDER).transpose(1, 3, 0, 2, 4)
    value = value.reshape(16 * inner, OUTER_ORDER * INNER_ORDER)
    value = jnp.dot(value, table, preferred_element_type=f32) * norm
    return value.reshape(16, inner, OUTER_ORDER * INNER_ORDER)


def to_shards(value):
    inner = value.shape[1]
    value = value.reshape(16, inner, NZ, 2, INNER_ORDER).transpose(2, 0, 3, 1, 4)
    return value.reshape(NZ * 16, 2 * inner * INNER_ORDER)


def to_tokens(gate_pre, up_pre, column_local):
    gate_value = gate_pre.astype(f32)
    hidden = (gate_value * jax.nn.sigmoid(gate_value) * up_pre.astype(f32)).astype(bf16)
    count = column_local.shape[0] // INNER_ORDER
    digits = []
    rest = column_local
    for _ in range(3):
        digit = lax.reduce_precision(rest, 8, 7)
        digits.append(digit.reshape(count, INNER_ORDER))
        rest = rest - digit
    digits = jnp.concatenate(digits, axis=0).astype(bf16)
    digits = jnp.pad(digits, ((0, 16 - 3 * count), (0, 0)))
    digits = jnp.broadcast_to(digits[None], (NZ, 16, INNER_ORDER)).reshape(-1, INNER_ORDER)
    sent = jnp.concatenate([hidden, digits], axis=1)
    sent = lax.all_to_all(sent, "z", 0, 0, tiled=True)
    got = sent.reshape(NZ, 16, -1)[:, : 3 * count, hidden.shape[1] :].astype(f32)
    got = got.reshape(NZ, 3, count * INNER_ORDER)
    return got[:, 0] + got[:, 1] + got[:, 2], sent


def local(gate_pre, up_pre, w_down, out_grad, outlier_ids):
    tok_rows, width = gate_pre.shape
    columns = w_down.shape[1]
    inner = width // (2 * INNER_ORDER)
    y, x, c, z = (lax.axis_index(a) for a in ("y", "x", "c", "z"))
    first = lax.shift_right_logical(x, 1) == 0
    even = c == 0
    table = jnp.asarray(np.kron(sylvester(OUTER_ORDER), sylvester(INNER_ORDER)), bf16)

    lanes = jnp.arange(INNER_ORDER, dtype=jnp.int32)
    groups = jnp.arange(NZ * width // INNER_ORDER, dtype=jnp.int32)
    high = (groups[:, None] == (outlier_ids // INNER_ORDER)[None, :]).astype(bf16)
    low = ((outlier_ids % INNER_ORDER)[:, None] == lanes[None, :]).astype(bf16)
    special = jnp.dot(high, low, preferred_element_type=f32)
    special_rows = lax.dynamic_index_in_dim(special.reshape(NZ, width), z, 0, keepdims=False)
    special_rows = special_rows.reshape(width, 1)
    special_mixed = special.reshape(NZ, 2, inner, INNER_ORDER).transpose(2, 0, 1, 3)
    special_mixed = special_mixed.reshape(1, inner, OUTER_ORDER * INNER_ORDER) != 0.0

    column_local = jnp.max(jnp.where(special_rows == 0.0, jnp.abs(w_down), 0.0), axis=0)
    peaks, sent = to_tokens(gate_pre, up_pre, column_local)

    own_grad = out_grad.reshape(2, 2, 2, 64, columns).transpose(2, 0, 1, 3, 4)
    own_grad = own_grad.reshape(8, 64, columns)
    own_grad, sent = lax.optimization_barrier((own_grad, sent))
    own_grad = lax.all_to_all(own_grad, ("x", "c"), split_axis=0, concat_axis=0, tiled=True)
    own_grad = rolled(own_grad.reshape(NX, NC, 64, columns), x)
    near_grad = jnp.where(even, own_grad[:, 0], own_grad[:, 1])
    far_grad = jnp.where(even, own_grad[:, 1], own_grad[:, 0])
    own_grad = jnp.concatenate([near_grad, far_grad], axis=0)
    own_grad = own_grad.transpose(1, 0, 2).reshape(64, 8 * columns)

    column_scale = ((jnp.max(peaks, axis=0) + epsilon) / levels)[None, :]
    softened, slope_w = soft_pair(w_down, column_scale, 1.0 / column_scale)
    quant_w = jnp.where(special_rows == 0.0, softened, w_down).astype(bf16)
    slope_w = jnp.where(special_rows == 0.0, slope_w, 1.0)
    sent, quant_w, own_grad = lax.optimization_barrier((sent, quant_w, own_grad))
    near = [quant_w] + [shift(quant_w, "x", NX, d) for d in (1, 2, 3)]

    half = 4 * columns
    ups, downs = [own_grad], [own_grad]
    for _ in range(3):
        ups.append(shift(ups[-1], "z", NZ, 1))
        downs.append(shift(downs[-1], "z", NZ, -1))
    middle = jnp.concatenate(
        [shift(ups[3][:, :half], "z", NZ, 1), shift(downs[3][:, half:], "z", NZ, -1)], axis=1
    )
    held_grad = jnp.concatenate([*ups, middle, downs[3], downs[2], downs[1]], axis=0)

    rotated = mixed(sent[:, :width], table)
    token_peak = jnp.max(
        jnp.where(special_mixed, 0.0, jnp.abs(rotated)), axis=(1, 2), keepdims=True
    )
    token_scale = (token_peak + epsilon) / levels
    softened, slope_act = soft_pair(rotated, token_scale, 1.0 / token_scale)
    quant_act = jnp.where(special_mixed, rotated, softened).astype(bf16)
    slope_act = jnp.where(special_mixed, 1.0, slope_act)
    quant_act = to_shards(quant_act)
    quant_act = lax.all_to_all(quant_act, "z", 0, 0, tiled=True)
    quant_act = quant_act.reshape(2, 64, width)
    quant_act, near, _ = lax.optimization_barrier((quant_act, near, (ups, downs)))
    near_w = jnp.concatenate(near, axis=1)
    far_w = shift(near_w, "c", NC, 1)

    pairs = [(i, i ^ 2) for i in range(NX)]
    mine = jnp.where(first, quant_act[0], quant_act[1])
    other = lax.ppermute(jnp.where(first, quant_act[1], quant_act[0]), "x", pairs)
    mine, other = jnp.where(first, mine, other), jnp.where(first, other, mine)
    joined = jnp.concatenate([mine, other], axis=0)
    rows_by_rows = (((1,), (1,)), ((), ()))
    share = lax.dot_general(
        held_grad[:, :half], near_w, rows_by_rows, preferred_element_type=f32
    ) + lax.dot_general(
        held_grad[:, half:], far_w, rows_by_rows, preferred_element_type=f32
    )
    share = share.astype(bf16)
    share = rolled(share.reshape(NZ, 64, width), NZ - z).reshape(NY, 128, width)
    late, share = lax.optimization_barrier((joined, share))
    share = lax.all_to_all(share, "y", 0, 0, tiled=True)
    acts = [joined, shift(joined, "y", NY, 1), shift(late, "y", NY, 2), shift(joined, "y", NY, 3)]
    acts = jnp.concatenate(acts, axis=0).reshape(NZ, 64, width)
    acts = rolled(acts, z + NZ - 2 * y).reshape(512, width)

    share = share.astype(f32)
    total = (share[0] + share[1] + share[2] + share[3]).astype(bf16).reshape(2, 64, width)
    mine = jnp.where(first, total[0], total[1])
    other = lax.ppermute(jnp.where(first, total[1], total[0]), "x", pairs)
    mine, other = jnp.where(first, mine, other), jnp.where(first, other, mine)
    act_grad = jnp.concatenate([mine, other], axis=0)
    acts, act_grad = lax.optimization_barrier((acts, act_grad))
    act_grad = lax.all_to_all(act_grad, "z", 0, 0, tiled=True)

    parts = []
    for cut in (slice(half, None), slice(0, half)):
        part = lax.dot_general(
            acts, held_grad[:, cut], (((0,), (0,)), ((), ())), preferred_element_type=f32
        )
        parts.append(part.astype(bf16))
    far_part, near_part = shift(parts[0], "c", NC, 1), parts[1]
    acts, near_part = lax.optimization_barrier((acts, near_part))

    partial = jnp.concatenate(
        [jnp.dot(acts, w, preferred_element_type=f32).astype(bf16) for w in (near_w, far_w)],
        axis=1,
    )
    partial = partial.reshape(NZ, 64, 8 * columns)
    cuts = [slice(d * columns, (d + 1) * columns) for d in range(4)]
    terms = [
        (near_part[:, cut].astype(f32) + far_part[:, cut].astype(f32)).astype(bf16)
        for cut in cuts[1:]
    ]
    partial, terms, act_grad = lax.optimization_barrier((partial, terms, act_grad))
    terms = [shift(term, "x", NX, -d) for d, term in zip((1, 2, 3), terms)]

    act_grad = act_grad.reshape(NZ, 16, 2, inner, INNER_ORDER).transpose(1, 3, 0, 2, 4)
    act_grad = act_grad.reshape(16, inner, OUTER_ORDER * INNER_ORDER).astype(f32)
    rot_grad = (act_grad * slope_act).astype(bf16)
    rot_grad = rot_grad.reshape(16 * inner, OUTER_ORDER * INNER_ORDER)
    hidden_grad = jnp.dot(rot_grad, table, preferred_element_type=f32) * norm
    hidden_grad = to_shards(hidden_grad.astype(bf16).reshape(16, inner, -1))

    low_part = shift(partial[4][:, :half], "z", NZ, -1).astype(f32)
    high_part = shift(partial[4][:, half:], "z", NZ, 1).astype(f32)
    zero = jnp.zeros_like(low_part)
    below = jnp.concatenate([low_part, zero], axis=1)
    above = jnp.concatenate([zero, high_part], axis=1)
    for d in (3, 2, 1):
        below = (partial[d].astype(f32) + below).astype(bf16)
        if d == 2:
            below, hidden_grad = lax.optimization_barrier((below, hidden_grad))
            hidden_grad = lax.all_to_all(hidden_grad, "z", 0, 0, tiled=True)
            below, terms[0], terms[2] = lax.optimization_barrier((below, terms[0], terms[2]))
        below = shift(below, "z", NZ, -1).astype(f32)
        above = shift((partial[8 - d].astype(f32) + above).astype(bf16), "z", NZ, 1).astype(f32)
    output = (partial[0].astype(f32) + below + above).astype(bf16)
    output = output.reshape(64, 8, columns).transpose(1, 0, 2)
    near_out, far_out = output[:4], output[4:]
    output = jnp.stack(
        [jnp.where(even, near_out, far_out), jnp.where(even, far_out, near_out)], axis=1
    )
    output = rolled(output, NX - x).reshape(8, 64, columns)
    output, hidden_grad, terms[1] = lax.optimization_barrier((output, hidden_grad, terms[1]))
    hidden_grad = hidden_grad.astype(f32)
    output = lax.all_to_all(output, ("x", "c"), split_axis=0, concat_axis=0, tiled=True)
    output = output.reshape(2, 2, 2, 64, columns).transpose(1, 2, 0, 3, 4).reshape(512, columns)

    gate_value = gate_pre.astype(f32)
    sigmoid_gate = jax.nn.sigmoid(gate_value)
    silu_slope = sigmoid_gate * (1.0 + gate_value * (1.0 - sigmoid_gate))
    gate_grad = (hidden_grad * up_pre.astype(f32) * silu_slope).astype(bf16)
    up_grad = (hidden_grad * (gate_value * sigmoid_gate)).astype(bf16)
    raw = near_part[:, cuts[0]].astype(f32) + far_part[:, cuts[0]].astype(f32)
    for term in terms:
        raw = raw + term.astype(f32)
    weight_grad = raw * slope_w
    return (output, weight_grad, gate_grad, up_grad)


def solution(mesh):
    grid = Mesh(mesh.devices.reshape(NY, NX, NC, NZ), ("y", "x", "c", "z"))
    rows, cols = P(("y", "x", "c"), "z"), P("z", ("y", "x", "c"))
    return jax.shard_map(
        local,
        mesh=grid,
        in_specs=(rows, rows, cols, cols, P()),
        out_specs=(cols, cols, rows, rows),
        check_vma=False,
    )
```
